32 devices in a mesh: groups: 2 (over x), mesh: 16 (over z, y, core).
Axes of the slice: x: 2, y: 2, z: 4, core: 2. Of those that a mesh axis runs over, the one named last changes fastest.
Arguments:
- node_feat: bfloat16 [32768, 256], P(('groups', 'mesh')), parts along dimension 0, may hold values from -6 to 6
- coarse_feat: bfloat16 [8192, 256], P(('groups', 'mesh')), parts along dimension 0, may hold values from -6 to 6
- neighbors: int32 [16384, 6], P('mesh'), may hold values from 0 to 16383, as said below
- up_owner: int32 [16384, 1], P('mesh'), may hold values from 0 to 15; in each aligned block of 1024 rows (0 to 1023, 1024 to 2047, ...) at most 128 rows name the same one
- up_local: int32 [16384], P('mesh'), may hold values from 0 to 255
- w_src: bfloat16 [2, 256, 256], replicated, may hold values from -0.375 to 0.375
- w_dst: bfloat16 [2, 256, 256], replicated, may hold values from -0.375 to 0.375
- w_node: bfloat16 [2, 256, 256], replicated, may hold values from -0.375 to 0.375
- w_edge: bfloat16 [2, 256, 256], replicated, may hold values from -0.15625 to 0.15625
- w_mix: bfloat16 [2, 256, 256], replicated, may hold values from -0.375 to 0.375
- edge_bias: float32 [2, 256], replicated, may hold values from -4 to 4
- w_up: bfloat16 [256, 256], replicated, may hold values from -0.375 to 0.375
- w_coarse: bfloat16 [256, 256], replicated, may hold values from -0.375 to 0.375
- w_down: bfloat16 [256, 256], replicated, may hold values from -0.375 to 0.375
Outputs:
- fine_out: bfloat16 [32768, 256], P(('groups', 'mesh')), parts along dimension 0
- coarse_out: bfloat16 [8192, 256], P(('groups', 'mesh')), parts along dimension 0
The draws below stay inside these ranges and needn't reach their ends.
There are 2 independent parts, one for each index of `groups`. The reference program is written for one: setup_inputs(seed, part) draws one part's arguments, and reference() takes and returns one part's arrays. A program takes and returns all parts, laid end to end along the dimension named above; an argument that names none is the same for every part. Nothing has to cross between parts.
Inputs may be any that keep to these rules, and one draw needn't show every extreme that they name: `neighbors`: entry (i, k) is (i + o) modulo 16384 with o between -128 and 128 and never 0; the offsets 128 and -128 both occur. `up_owner`: among the 1024 rows of one device no owner is named more than 128 times, a bound that some block reaches.
All inputs are finite; a program needn't handle non-finite values.
Results may differ from the reference program's by a relative error of at most 0.0071.
Values may be sent and summed in bfloat16 or wider, within the bound.
A program may use at most 64 MiB of HBM per device.

```python
import math
import jax
import jax.numpy as jnp
import numpy as np

D = 256
K = 6
R = 128
ROUNDS = 2
F_DEV = 1024
C_DEV = 256
CAP = 128
FINE = 16384
COARSE = 4096
N_MESH = 16


def draw_neighbors(key, part):
    key = jax.random.fold_in(key, 11)
    key_size, key_sign = jax.random.split(key)
    magnitude = jax.random.randint(key_size, (FINE, K), 1, R + 1)
    signs = jax.random.randint(key_sign, (FINE, K), 0, 2) * 2 - 1
    offsets = (magnitude * signs).astype(jnp.int32)
    offsets = offsets.at[0, 0].set(R).at[1, 0].set(-R)
    positions = jnp.arange(FINE, dtype=jnp.int32)[:, None]
    return jnp.mod(positions + offsets, FINE).astype(jnp.int32)


def with_ends(entries, key, smallest, top_value):
    dims = entries.shape
    index_at = [jax.random.randint(jax.random.fold_in(key, axis), (), 0, dims[axis]) for axis in range(len(dims))]
    entries = entries.at[tuple(index_at)].set(smallest)
    longest = dims.index(max(dims))
    index_at[longest] = (index_at[longest] + 1) % dims[longest]
    return entries.at[tuple(index_at)].set(top_value)


def shard_levels(stream_key, shape, pieces, least, high):
    level, own = 1.0, jax.random.fold_in(stream_key, 6)
    for dim, blocks in pieces:
        steps = jnp.exp(jax.random.uniform(jax.random.fold_in(own, dim), (blocks,), jnp.float32, least / len(pieces), high / len(pieces)))
        level = level * jnp.repeat(steps, shape[dim] // blocks).reshape([-1 if axis == dim else 1 for axis in range(len(shape))])
    return level


def shared_out(rng, own, number, rows, number_of, top, most, skew):
    ranking = jax.random.permutation(rng, number_of)
    crowded, ordinary = portions_of(number_of, rows * top, most, skew, True), portions_of(number_of, rows * top, most, skew, False)
    places = jnp.arange(number_of)

    def named(sizes, offset_by):
        used = int((sizes > 0).sum())
        fixed = max(1, used // 4)
        moved = fixed + (places - fixed + offset_by * (used - fixed)) % max(1, number_of - fixed)
        return jnp.zeros((number_of,), jnp.int32).at[ranking[jnp.where(places < fixed, places, moved)]].set(jnp.asarray(sizes, jnp.int32))

    sizes = jnp.where(number % 4 == 0, named(crowded, number // 4), named(ordinary, number - number // 4 - 1))
    mixed = jax.random.permutation(jax.random.fold_in(own, 3), number_of)
    giver, taker = mixed[0:number_of // 2 * 2:2], mixed[1:number_of // 2 * 2:2]
    slack = jnp.minimum(sizes[giver] - 1, most - sizes[taker]) // 2
    slack = jnp.where((giver == ranking[0]) | (taker == ranking[0]) | (sizes[taker] == 0), 0, jnp.maximum(slack, 0))
    moved = jax.random.randint(jax.random.fold_in(own, 4), (number_of // 2,), 0, 1 << 20) % (slack + 1)
    sizes = sizes.at[giver].add(-moved).at[taker].add(moved)
    members = jnp.searchsorted(jnp.cumsum(sizes), jnp.arange(rows * top), side="right").astype(jnp.int32)
    listing = members.reshape(top, rows).T
    listing = listing[jax.random.permutation(jax.random.fold_in(own, 1), rows)]
    offset_by = jax.random.randint(jax.random.fold_in(own, 2), (rows, 1), 0, top)
    return jnp.take_along_axis(listing, (jnp.arange(top)[None, :] + offset_by) % top, axis=1)


def portions_of(count, total, bound, slope, full):
    loads = [(1 << 20) // math.isqrt(standing ** slope) + 1 for standing in range(1, count + 1)]
    largest = bound if full else min(bound, max(-(-total // count), total * loads[0] // sum(loads)))
    least = 1 if total - largest >= count - 1 else 0
    counts, spare = [largest] + [least] * (count - 1), total - largest - least * (count - 1)
    while spare > 0:
        free = [i for i in range(1, count) if counts[i] < largest] or [i for i in range(1, count) if counts[i] < bound]
        whole, remaining = sum([loads[i] for i in free]), spare
        for i in free:
            addition = min(bound - counts[i], max(1, remaining * loads[i] // whole), spare)
            counts[i] = counts[i] + addition
            spare = spare - addition
    return np.array(counts)


def normal_values(own_key, dims, spread, bound, cuts=(), kind=jnp.bfloat16):
    entries = jax.random.normal(own_key, dims, jnp.float32) * spread
    if len(cuts) > 0:
        entries = shard_levels(own_key, dims, cuts, -0.22, 0.18) * entries
    return jnp.clip(entries, min=-bound, max=bound).astype(kind)


def setup_inputs(seed: int = 0, part: int = 0) -> dict:
    seeds = jax.random.split(jax.random.key(seed), 15)
    part_splits = jax.random.split(jax.random.fold_in(seeds[14], part), 15)
    node_feat = normal_values(part_splits[0], (FINE, D), 1.0, 6.0, ((0, 16),))
    coarse_feat = normal_values(part_splits[1], (COARSE, D), 1.0, 6.0, ((0, 16),))
    neighbors = draw_neighbors(jax.random.fold_in(seeds[14], 71), part)
    up_owner_keys = jax.random.split(jax.random.fold_in(seeds[3], 1), FINE // F_DEV)
    up_owner_turns = jax.random.permutation(jax.random.fold_in(seeds[3], 3), FINE // F_DEV)
    up_owner = jax.vmap(lambda own, number: shared_out(jax.random.fold_in(seeds[3], 2), own, number, F_DEV, N_MESH, 1, CAP, 2))(up_owner_keys, up_owner_turns).reshape((FINE, 1))
    up_local = with_ends(jax.random.randint(seeds[4], (FINE,), 0, C_DEV), jax.random.fold_in(seeds[4], 1), 0, C_DEV - 1).astype(jnp.int32)
    w_src = normal_values(seeds[5], (ROUNDS, D, D), D ** -0.5, 0.375)
    w_dst = normal_values(seeds[6], (ROUNDS, D, D), D ** -0.5, 0.375)
    w_node = normal_values(seeds[7], (ROUNDS, D, D), D ** -0.5, 0.375)
    w_edge = normal_values(seeds[8], (ROUNDS, D, D), (K * D) ** -0.5, 0.15625)
    w_mix = normal_values(seeds[9], (ROUNDS, D, D), D ** -0.5, 0.375)
    edge_bias = normal_values(seeds[10], (ROUNDS, D), 1.0, 4.0, (), jnp.float32)
    w_up = normal_values(seeds[11], (D, D), D ** -0.5, 0.375)
    w_coarse = normal_values(seeds[12], (D, D), D ** -0.5, 0.375)
    w_down = normal_values(seeds[13], (D, D), D ** -0.5, 0.375)
    return {"node_feat": node_feat, "coarse_feat": coarse_feat, "neighbors": neighbors, "up_owner": up_owner, "up_local": up_local, "w_src": w_src, "w_dst": w_dst, "w_node": w_node, "w_edge": w_edge, "w_mix": w_mix, "edge_bias": edge_bias, "w_up": w_up, "w_coarse": w_coarse, "w_down": w_down}


def reference(node_feat, coarse_feat, neighbors, up_owner, up_local, w_src, w_dst, w_node, w_edge, w_mix, edge_bias, w_up, w_coarse, w_down):
    hidden_width = node_feat
    for round_index in range(ROUNDS):
        src_term = jnp.dot(hidden_width, w_src[round_index], preferred_element_type=jnp.float32)
        dst_term = jnp.dot(hidden_width, w_dst[round_index], preferred_element_type=jnp.float32).astype(jnp.bfloat16)
        biased = src_term + edge_bias[round_index].astype(jnp.float32)[None, :]
        edge_sum = jnp.zeros(src_term.shape, jnp.float32)
        for edge_index in range(K):
            edge_sum = edge_sum + jax.nn.silu(biased + dst_term[neighbors[:, edge_index]].astype(jnp.float32))
        node_update = jax.nn.silu(jnp.dot(hidden_width, w_node[round_index], preferred_element_type=jnp.float32) + jnp.dot(edge_sum.astype(jnp.bfloat16), w_edge[round_index], preferred_element_type=jnp.float32)).astype(jnp.bfloat16)
        hidden_width = (hidden_width.astype(jnp.float32) + jnp.dot(node_update, w_mix[round_index], preferred_element_type=jnp.float32)).astype(jnp.bfloat16)
    message = jax.nn.silu(jnp.dot(hidden_width, w_up, preferred_element_type=jnp.float32)).astype(jnp.bfloat16)
    parent = (up_owner[:, 0] * C_DEV + up_local).astype(jnp.int32)
    summed = jax.ops.segment_sum(message.astype(jnp.float32), parent, COARSE)
    child_count = jax.ops.segment_sum(jnp.ones(parent.shape, jnp.float32), parent, COARSE)
    coarse_mean = (summed / jnp.maximum(child_count, 1.0)[:, None]).astype(jnp.bfloat16)
    coarse_out = (coarse_feat.astype(jnp.float32) + jnp.dot(coarse_mean, w_coarse, preferred_element_type=jnp.float32)).astype(jnp.bfloat16)
    parent_feat = coarse_out[parent]
    fine_out = (hidden_width.astype(jnp.float32) + jnp.dot(parent_feat, w_down, preferred_element_type=jnp.float32)).astype(jnp.bfloat16)
    return fine_out, coarse_out
```

```python
import functools

import jax
import jax.numpy as jnp
from jax import lax
from jax.experimental import pallas as pl
from jax.experimental.pallas import tpu as pltpu
from jax.sharding import PartitionSpec as P

R = 128
ROUNDS = 2
BLOCK = 128
BF = jnp.bfloat16
F32 = jnp.float32


def dot(a, b):
    return jnp.dot(a, b, preferred_element_type=F32)


def silu(x):
    h = 0.5 * x
    return h + h * jnp.tanh(h)


def kernel(
    n,
    x_ref,
    cf_ref,
    nb_ref,
    pc_ref,
    pr_ref,
    w_src,
    w_dst,
    w_node,
    w_edge,
    w_mix,
    bias_ref,
    w_up,
    w_coarse,
    w_down,
    fine_ref,
    coarse_ref,
    pick,
    ext,
    srch,
    esum,
    hid,
    msg,
    sib_row,
    hist,
    counts,
    sbuf,
    rbuf,
    gath,
    acc,
    halo_s,
    halo_r,
    cnt_s,
    cnt_r,
    row_s,
    row_r,
    msg_s,
    msg_r,
    red_s,
    red_r,
    ag_s,
    ag_r,
    sib_s,
    sib_r,
):
    rows, width = x_ref.shape
    edges = nb_ref.shape[1]
    cells = cf_ref.shape[0]
    half = cells // 2
    blocks = rows // BLOCK
    window = BLOCK + 2 * R
    ring = n // 2
    total = rows * n
    me = lax.axis_index("mesh")
    core = me % 2
    sibling = me + 1 - 2 * core
    chip = me // 2
    span = ring // 2
    pos = jnp.where(chip % 2 == 0, chip // 2, ring - 1 - chip // 2)

    def owner_at(place):
        place = (place + 2 * ring) % ring
        return jnp.where(place < span, 2 * place, 2 * (ring - 1 - place) + 1) * 2

    right = owner_at(pos + 1) + core
    left = owner_at(pos - 1) + core
    after = (me + 1) % n
    before = (me + n - 1) % n

    def remote(src, dst, ssem, rsem, dev):
        return pltpu.make_async_remote_copy(
            src_ref=src,
            dst_ref=dst,
            send_sem=ssem,
            recv_sem=rsem,
            device_id={"mesh": dev},
            device_id_type=pl.DeviceIdType.MESH,
        )

    barrier = pltpu.get_barrier_semaphore()

    def greet(j, c):
        pl.semaphore_signal(
            barrier,
            inc=1,
            device_id={"mesh": (me + j) % n},
            device_id_type=pl.DeviceIdType.MESH,
        )
        return c

    lax.fori_loop(1, n, greet, 0)

    ext[0, pl.ds(R, rows), :] = dot(x_ref[...], w_dst[0]).astype(BF)
    lows = (lax.broadcasted_iota(jnp.int32, (8 * n, 1), 0) // 8) * cells
    parents = pr_ref[...]
    owner_hot = jnp.where((parents >= lows) & (parents < lows + cells), 1.0, 0.0).astype(BF)
    local = jnp.bitwise_and(pc_ref[...], cells - 1)
    local_hot = jnp.where(
        local == lax.broadcasted_iota(jnp.int32, (rows, cells), 1), 1.0, 0.0
    ).astype(BF)
    hist[...] = dot(owner_hot, local_hot)

    pl.semaphore_wait(barrier, n - 1)

    def halo(l):
        return (
            remote(
                ext.at[l, pl.ds(R, R)],
                ext.at[l, pl.ds(R + rows, R)],
                halo_s.at[l, 0],
                halo_r.at[l, 0],
                before,
            ),
            remote(
                ext.at[l, pl.ds(rows, R)],
                ext.at[l, pl.ds(0, R)],
                halo_s.at[l, 1],
                halo_r.at[l, 1],
                after,
            ),
        )

    for c in halo(0):
        c.start()
    row_copy = remote(pr_ref, sib_row, row_s, row_r, sibling)
    row_copy.start()

    def count_copy(peer, slot):
        return remote(
            hist.at[pl.ds(peer * 8, 8)],
            counts.at[pl.ds(slot * 8, 8)],
            cnt_s.at[peer],
            cnt_r.at[slot],
            peer,
        )

    def send_counts(j, c):
        count_copy((me + j) % n, me).start()
        return c

    lax.fori_loop(1, n, send_counts, 0)

    def build(b, c):
        r0 = b * BLOCK
        rel = nb_ref[pl.ds(r0, BLOCK), :] - (me * rows - R)
        rel = jnp.where(rel < 0, rel + total, rel)
        rel = jnp.where(rel >= total, rel - total, rel) - r0
        lanes = lax.broadcasted_iota(jnp.int32, (BLOCK, window), 1)
        for k in range(edges):
            pick[b, pl.ds(k * BLOCK, BLOCK), :] = jnp.where(
                rel[:, k : k + 1] == lanes, 0.5, 0.0
            ).astype(BF)
        return c

    def edge_block(l, b):
        r0 = b * BLOCK
        if l == 0:
            build(b, 0)
        sel = dot(pick[b], ext[l, pl.ds(r0, window), :])
        base = srch[pl.ds(r0, BLOCK), :]
        out = jnp.zeros((BLOCK, width), F32)
        for k in range(edges):
            h = base + sel[k * BLOCK : (k + 1) * BLOCK]
            out = out + (h + h * jnp.tanh(h))
        esum[pl.ds(r0, BLOCK), :] = out.astype(BF)

    chunk = rows // 4

    def msg_copy(i):
        part = pl.ds(i * chunk, chunk)
        return remote(msg.at[0, part], msg.at[1, part], msg_s.at[i], msg_r.at[i], sibling)

    for l in range(ROUNDS):
        here = x_ref if l == 0 else hid
        srch[...] = 0.5 * (dot(here[...], w_src[l]) + bias_ref[l : l + 1, :])

        def inner(b, c, l=l):
            edge_block(l, b)
            return c

        lax.fori_loop(1, blocks - 1, inner, 0)
        for c in halo(l):
            c.wait_recv()

        def outer(j, c, l=l):
            edge_block(l, j * (blocks - 1))
            return c

        lax.fori_loop(0, 2, outer, 0)
        for i in range(4):
            part = pl.ds(i * chunk, chunk)
            old = here[part, :]
            upd = silu(dot(old, w_node[l]) + dot(esum[part, :], w_edge[l])).astype(BF)
            new = (old.astype(F32) + dot(upd, w_mix[l])).astype(BF)
            hid[part, :] = new
            if l + 1 < ROUNDS:
                ext[l + 1, pl.ds(R + i * chunk, chunk), :] = dot(new, w_dst[l + 1]).astype(BF)
            else:
                msg[0, part, :] = silu(dot(new, w_up[...])).astype(BF)
                msg_copy(i).start()
        if l + 1 < ROUNDS:
            for c in halo(l + 1):
                c.start()

    counts[pl.ds(pl.multiple_of(me * 8, 8), 8), :] = hist[pl.ds(pl.multiple_of(me * 8, 8), 8), :]

    def take_counts(j, c):
        count_copy(me, (me + j) % n).wait_recv()
        return c

    lax.fori_loop(1, n, take_counts, 0)
    number = jnp.zeros((8, cells), F32)
    for j in range(n):
        number = number + counts[j * 8 : (j + 1) * 8, :]
    diag = lax.broadcasted_iota(jnp.int32, (cells, cells), 0) == lax.broadcasted_iota(
        jnp.int32, (cells, cells), 1
    )
    number = jnp.sum(jnp.where(diag, number[0:1, :], 0.0), axis=1, keepdims=True)
    scale = 1.0 / jnp.maximum(number, 1.0)

    row_copy.wait_recv()
    for i in range(4):
        msg_copy(i).wait_recv()

    cell_iota = lax.broadcasted_iota(jnp.int32, (cells, 1), 0)

    def partial_sums(s):
        low = (owner_at(pos - 1 - s) + core) * cells
        high = (owner_at(pos + 1 + s) + core) * cells
        ids = cell_iota + jnp.where(cell_iota < half, low, high)
        mine = jnp.where(pr_ref[...] == ids, 1.0, 0.0).astype(BF)
        theirs = jnp.where(sib_row[...] == ids, 1.0, 0.0).astype(BF)
        return dot(mine, msg[0]) + dot(theirs, msg[1])

    def red_copy(d, s):
        return remote(
            sbuf.at[s, d],
            rbuf.at[s, d],
            red_s.at[s, d],
            red_r.at[s, d],
            right if d == 0 else left,
        )

    first = partial_sums(0)
    for d in range(2):
        sbuf[0, d] = first[d * half : (d + 1) * half].astype(BF)
        red_copy(d, 0).start()

    def reduce_step(s, c):
        part = partial_sums(s)
        for d in range(2):
            red_copy(d, s - 1).wait_recv()
            sbuf[s, d] = (
                part[d * half : (d + 1) * half] + rbuf[s - 1, d].astype(F32)
            ).astype(BF)
            red_copy(d, s).start()
        return c

    lax.fori_loop(1, ring - 1, reduce_step, 0)
    part = partial_sums(ring - 1)
    for d in range(2):
        red_copy(d, ring - 2).wait_recv()
        side = slice(d * half, (d + 1) * half)
        summed = part[side] + rbuf[ring - 2, d].astype(F32)
        mean = (summed * scale[side]).astype(BF)
        out = (cf_ref[side, :].astype(F32) + dot(mean, w_coarse[...])).astype(BF)
        coarse_ref[side, :] = out
        gath[0, 0, d] = out

    def ag_copy(d, s):
        return remote(
            gath.at[0, s, d],
            gath.at[0, s + 1, d],
            ag_s.at[s, d],
            ag_r.at[s, d],
            right if d == 0 else left,
        )

    def sib_copy(s):
        return remote(gath.at[0, s], gath.at[1, s], sib_s.at[s], sib_r.at[s], sibling)

    lane_iota = lax.broadcasted_iota(jnp.int32, (1, cells), 1)

    def gather(s):
        low = owner_at(pos - s)
        high = owner_at(pos + s)
        ids = lane_iota + jnp.where(lane_iota < half, low, high) * cells
        mine = ids + core * cells
        theirs = ids + (1 - core) * cells
        column = pc_ref[...]
        hot = jnp.where(column == mine, 1.0, 0.0).astype(BF)
        got = dot(hot, gath[0, s].reshape(cells, width))
        sib_copy(s).wait_recv()
        hot = jnp.where(column == theirs, 1.0, 0.0).astype(BF)
        return got + dot(hot, gath[1, s].reshape(cells, width))

    for d in range(2):
        ag_copy(d, 0).start()
    sib_copy(0).start()
    acc[...] = gather(0)

    def gather_step(s, c):
        for d in range(2):
            ag_copy(d, s - 1).wait_recv()
            ag_copy(d, s).start()
        sib_copy(s).start()
        acc[...] += gather(s)
        return c

    lax.fori_loop(1, ring - 1, gather_step, 0)
    for d in range(2):
        ag_copy(d, ring - 2).wait_recv()
    sib_copy(ring - 1).start()
    found = (acc[...] + gather(ring - 1)).astype(BF)
    fine_ref[...] = (hid[...].astype(F32) + dot(found, w_down[...])).astype(BF)

    for l in range(ROUNDS):
        for c in halo(l):
            c.wait_send()
    row_copy.wait_send()
    for i in range(4):
        msg_copy(i).wait_send()

    def drain_counts(j, c):
        count_copy((me + j) % n, me).wait_send()
        return c

    lax.fori_loop(1, n, drain_counts, 0)

    def drain_ring(s, c):
        for d in range(2):
            red_copy(d, s).wait_send()
            ag_copy(d, s).wait_send()
        sib_copy(s).wait_send()
        return c

    lax.fori_loop(0, ring - 1, drain_ring, 0)
    sib_copy(ring - 1).wait_send()


def shards(n, node_feat, coarse_feat, neighbors, up_owner, up_local, *weights):
    rows, width = node_feat.shape
    cells = coarse_feat.shape[0]
    edges = neighbors.shape[1]
    blocks = rows // BLOCK
    window = BLOCK + 2 * R
    ring = n // 2
    half = cells // 2
    parent = up_owner[:, 0] * cells + up_local
    dma = pltpu.SemaphoreType.DMA
    vmem = pl.BlockSpec(memory_space=pltpu.VMEM)
    return pl.pallas_call(
        functools.partial(kernel, n),
        out_shape=(
            jax.ShapeDtypeStruct((rows, width), BF),
            jax.ShapeDtypeStruct((cells, width), BF),
        ),
        in_specs=[vmem] * 14,
        out_specs=(vmem, vmem),
        scratch_shapes=[
            pltpu.VMEM((blocks, edges * BLOCK, window), BF),
            pltpu.VMEM((ROUNDS, rows + 2 * R, width), BF),
            pltpu.VMEM((rows, width), F32),
            pltpu.VMEM((rows, width), BF),
            pltpu.VMEM((rows, width), BF),
            pltpu.VMEM((2, rows, width), BF),
            pltpu.VMEM((1, rows), jnp.int32),
            pltpu.VMEM((8 * n, cells), F32),
            pltpu.VMEM((8 * n, cells), F32),
            pltpu.VMEM((ring - 1, 2, half, width), BF),
            pltpu.VMEM((ring - 1, 2, half, width), BF),
            pltpu.VMEM((2, ring, 2, half, width), BF),
            pltpu.VMEM((rows, width), F32),
            dma((ROUNDS, 2)),
            dma((ROUNDS, 2)),
            dma((n,)),
            dma((n,)),
            dma,
            dma,
            dma((4,)),
            dma((4,)),
            dma((ring - 1, 2)),
            dma((ring - 1, 2)),
            dma((ring - 1, 2)),
            dma((ring - 1, 2)),
            dma((ring,)),
            dma((ring,)),
        ],
        compiler_params=pltpu.CompilerParams(
            collective_id=0, has_side_effects=True, vmem_limit_bytes=48 * 1024 * 1024
        ),
    )(
        node_feat,
        coarse_feat,
        neighbors,
        parent[:, None],
        parent[None, :],
        *weights,
    )


def solution(mesh):
    both = P(("groups", "mesh"), None)
    in_specs = (both, both, P("mesh", None), P("mesh", None), P("mesh")) + (P(),) * 9
    return jax.shard_map(
        functools.partial(shards, mesh.shape["mesh"]),
        mesh=mesh,
        in_specs=in_specs,
        out_specs=(both, both),
        check_vma=False,
    )
```

```python
import functools

import jax
import jax.numpy as jnp
from jax import lax
from jax.experimental import pallas as pl
from jax.experimental.pallas import tpu as pltpu
from jax.sharding import PartitionSpec as P

R = 128
ROUNDS = 2
BLOCK = 128
LOAD_ORDER = (0, 4, 3, 2, 8, 5, 6, 7, 9, 1, 10, 11)
BF = jnp.bfloat16
F32 = jnp.float32


def dot(a, b):
    return jnp.dot(a, b, preferred_element_type=F32)


def silu(x):
    h = 0.5 * x
    return h + h * jnp.tanh(h)


def kernel(
    n,
    pc_ref,
    pr_ref,
    *refs,
):
    given, (fine_ref, coarse_ref), held = refs[:12], refs[12:14], refs[14:26]
    sweep(n, pc_ref, pr_ref, given, held, *held, fine_ref, coarse_ref, *refs[26:])


def sweep(
    n,
    pc_ref,
    pr_ref,
    given,
    held,
    x_ref,
    cf_ref,
    nb_ref,
    w_src,
    w_dst,
    w_node,
    w_edge,
    w_mix,
    bias_ref,
    w_up,
    w_coarse,
    w_down,
    fine_ref,
    coarse_ref,
    load_s,
    pick,
    ext,
    srch,
    esum,
    hid,
    msg,
    sib_row,
    hist,
    counts,
    sbuf,
    rbuf,
    gath,
    acc,
    halo_s,
    halo_r,
    cnt_s,
    cnt_r,
    row_s,
    row_r,
    msg_s,
    msg_r,
    red_s,
    red_r,
    ag_s,
    ag_r,
    sib_s,
    sib_r,
):
    rows, width = x_ref.shape
    edges = nb_ref.shape[1]
    cells = cf_ref.shape[0]
    half = cells // 2
    blocks = rows // BLOCK
    window = BLOCK + 2 * R
    ring = n // 2
    total = rows * n
    me = lax.axis_index("mesh")
    core = me % 2
    sibling = me + 1 - 2 * core
    chip = me // 2
    span = ring // 2
    pos = jnp.where(chip % 2 == 0, chip // 2, ring - 1 - chip // 2)

    def owner_at(place):
        place = (place + 2 * ring) % ring
        return jnp.where(place < span, 2 * place, 2 * (ring - 1 - place) + 1) * 2

    right = owner_at(pos + 1) + core
    left = owner_at(pos - 1) + core
    after = (me + 1) % n
    before = (me + n - 1) % n

    def remote(src, dst, ssem, rsem, dev):
        return pltpu.make_async_remote_copy(
            src_ref=src,
            dst_ref=dst,
            send_sem=ssem,
            recv_sem=rsem,
            device_id={"mesh": dev},
            device_id_type=pl.DeviceIdType.MESH,
        )

    barrier = pltpu.get_barrier_semaphore()

    def greet(j, c):
        pl.semaphore_signal(
            barrier,
            inc=1,
            device_id={"mesh": (me + j) % n},
            device_id_type=pl.DeviceIdType.MESH,
        )
        return c

    loads = [pltpu.make_async_copy(a, b, load_s.at[i]) for i, (a, b) in enumerate(zip(given, held))]
    for i in LOAD_ORDER:
        loads[i].start()
    lax.fori_loop(1, n, greet, 0)
    for i in LOAD_ORDER:
        loads[i].wait()

    ext[0, pl.ds(R, rows), :] = dot(x_ref[...], w_dst[0]).astype(BF)
    lows = (lax.broadcasted_iota(jnp.int32, (8 * n, 1), 0) // 8) * cells
    parents = pr_ref[...]
    owner_hot = jnp.where((parents >= lows) & (parents < lows + cells), 1.0, 0.0).astype(BF)
    local = jnp.bitwise_and(pc_ref[...], cells - 1)
    local_hot = jnp.where(
        local == lax.broadcasted_iota(jnp.int32, (rows, cells), 1), 1.0, 0.0
    ).astype(BF)
    hist[...] = dot(owner_hot, local_hot)

    def build(b, c):
        r0 = b * BLOCK
        rel = nb_ref[pl.ds(r0, BLOCK), :] - (me * rows - R)
        rel = jnp.where(rel < 0, rel + total, rel)
        rel = jnp.where(rel >= total, rel - total, rel) - r0
        lanes = lax.broadcasted_iota(jnp.int32, (BLOCK, window), 1)
        for k in range(edges):
            pick[b, pl.ds(k * BLOCK, BLOCK), :] = jnp.where(
                rel[:, k : k + 1] == lanes, 0.5, 0.0
            ).astype(BF)
        return c

    def edge_block(l, b):
        r0 = b * BLOCK
        if l == 0:
            build(b, 0)
        sel = dot(pick[b], ext[l, pl.ds(r0, window), :])
        base = srch[pl.ds(r0, BLOCK), :]
        out = jnp.zeros((BLOCK, width), F32)
        for k in range(edges):
            h = base + sel[k * BLOCK : (k + 1) * BLOCK]
            out = out + (h + h * jnp.tanh(h))
        esum[pl.ds(r0, BLOCK), :] = out.astype(BF)

    def inner(l, low, high):
        def step(b, c):
            edge_block(l, b)
            return c

        lax.fori_loop(low, high, step, 0)

    def src_terms(l):
        here = x_ref if l == 0 else hid
        srch[...] = 0.5 * (dot(here[...], w_src[l]) + bias_ref[l : l + 1, :])

    early = 1 + (blocks - 2) // 2
    src_terms(0)
    inner(0, 1, early)

    pl.semaphore_wait(barrier, n - 1)

    def halo(l):
        return (
            remote(
                ext.at[l, pl.ds(R, R)],
                ext.at[l, pl.ds(R + rows, R)],
                halo_s.at[l, 0],
                halo_r.at[l, 0],
                before,
            ),
            remote(
                ext.at[l, pl.ds(rows, R)],
                ext.at[l, pl.ds(0, R)],
                halo_s.at[l, 1],
                halo_r.at[l, 1],
                after,
            ),
        )

    for c in halo(0):
        c.start()
    row_copy = remote(pr_ref, sib_row, row_s, row_r, sibling)
    row_copy.start()

    def count_copy(peer, slot):
        return remote(
            hist.at[pl.ds(peer * 8, 8)],
            counts.at[pl.ds(slot * 8, 8)],
            cnt_s.at[peer],
            cnt_r.at[slot],
            peer,
        )

    def send_counts(j, c):
        count_copy((me + j) % n, me).start()
        return c

    lax.fori_loop(1, n, send_counts, 0)

    chunk = rows // 4

    def msg_copy(i):
        part = pl.ds(i * chunk, chunk)
        return remote(msg.at[0, part], msg.at[1, part], msg_s.at[i], msg_r.at[i], sibling)

    for l in range(ROUNDS):
        here = x_ref if l == 0 else hid
        if l == 0:
            inner(0, early, blocks - 1)
        else:
            src_terms(l)
            inner(l, 1, blocks - 1)
        for c in halo(l):
            c.wait_recv()

        def outer(j, c, l=l):
            edge_block(l, j * (blocks - 1))
            return c

        lax.fori_loop(0, 2, outer, 0)
        for i in range(4):
            part = pl.ds(i * chunk, chunk)
            old = here[part, :]
            upd = silu(dot(old, w_node[l]) + dot(esum[part, :], w_edge[l])).astype(BF)
            new = (old.astype(F32) + dot(upd, w_mix[l])).astype(BF)
            hid[part, :] = new
            if l + 1 < ROUNDS:
                ext[l + 1, pl.ds(R + i * chunk, chunk), :] = dot(new, w_dst[l + 1]).astype(BF)
            else:
                msg[0, part, :] = silu(dot(new, w_up[...])).astype(BF)
                msg_copy(i).start()
        if l + 1 < ROUNDS:
            for c in halo(l + 1):
                c.start()

    counts[pl.ds(pl.multiple_of(me * 8, 8), 8), :] = hist[pl.ds(pl.multiple_of(me * 8, 8), 8), :]

    def take_counts(j, c):
        count_copy(me, (me + j) % n).wait_recv()
        return c

    lax.fori_loop(1, n, take_counts, 0)
    number = jnp.zeros((8, cells), F32)
    for j in range(n):
        number = number + counts[j * 8 : (j + 1) * 8, :]
    diag = lax.broadcasted_iota(jnp.int32, (cells, cells), 0) == lax.broadcasted_iota(
        jnp.int32, (cells, cells), 1
    )
    number = jnp.sum(jnp.where(diag, number[0:1, :], 0.0), axis=1, keepdims=True)
    scale = 1.0 / jnp.maximum(number, 1.0)

    row_copy.wait_recv()
    for i in range(4):
        msg_copy(i).wait_recv()

    far = ring // 2
    cell_iota = lax.broadcasted_iota(jnp.int32, (cells, 1), 0)
    parts = (slice(0, half), slice(half, cells))

    def partial_sums(place):
        ids = cell_iota + (owner_at(place) + core) * cells
        mine = jnp.where(pr_ref[...] == ids, 1.0, 0.0).astype(BF)
        theirs = jnp.where(sib_row[...] == ids, 1.0, 0.0).astype(BF)
        return dot(mine, msg[0]) + dot(theirs, msg[1])

    def red_copy(d, h, s):
        return remote(
            sbuf.at[s, d, h],
            rbuf.at[s, d, h],
            red_s.at[s, d, h],
            red_r.at[s, d, h],
            right if d == 0 else left,
        )

    def reduce_step(s, first):
        own = (partial_sums(pos + (far - s)), partial_sums(pos - (far - s)))
        pieces = ((0, 1), (1, 0), (0, 0), (1, 1))
        for d, h in pieces:
            part = own[d][parts[h]]
            if not (first and d != h):
                red_copy(d, h, s - 1).wait_recv()
                part = part + rbuf[s - 1, d, h].astype(F32)
            sbuf[s, d, h] = part.astype(BF)
            red_copy(d, h, s).start()

    part = partial_sums(pos + far)
    for d in range(2):
        sbuf[0, d, d] = part[parts[d]].astype(BF)
        red_copy(d, d, 0).start()
    reduce_step(1, True)

    def reduce_loop(s, c):
        reduce_step(s, False)
        return c

    lax.fori_loop(2, far, reduce_loop, 0)
    part = partial_sums(pos)

    def ag_copy(d, h, s, last=False):
        return remote(
            gath.at[0, s, d, h],
            gath.at[0, s + 1, 0 if last else d, h],
            ag_s.at[s, d, h],
            ag_r.at[s, d, h],
            right if d == 0 else left,
        )

    def sib_copy(s, d):
        return remote(gath.at[0, s, d], gath.at[1, s, d], sib_s.at[s, d], sib_r.at[s, d], sibling)

    for h in (1, 0):
        summed = part[parts[h]]
        for d in range(2):
            red_copy(d, h, far - 1).wait_recv()
            summed = summed + rbuf[far - 1, d, h].astype(F32)
        mean = (summed * scale[parts[h]]).astype(BF)
        out = (cf_ref[parts[h], :].astype(F32) + dot(mean, w_coarse[...])).astype(BF)
        gath[0, 0, 0, h] = out
        gath[0, 0, 1, h] = out
        ag_copy(0, h, 0).start()
        ag_copy(1, h, 0).start()
        coarse_ref[parts[h], :] = out
    sib_copy(0, 0).start()

    lane_iota = lax.broadcasted_iota(jnp.int32, (1, cells), 1)

    def gather(s, d, slot):
        owner = owner_at(pos - s if d == 0 else pos + s) + (core if slot == 0 else 1 - core)
        hot = jnp.where(pc_ref[...] == lane_iota + owner * cells, 1.0, 0.0).astype(BF)
        return dot(hot, gath[slot, s, d].reshape(cells, width))

    acc[...] = gather(0, 0, 0)
    sib_copy(0, 0).wait_recv()
    acc[...] += gather(0, 0, 1)

    def gather_step(s, last):
        for h in (1, 0):
            for d in range(2):
                ag_copy(d, h, s - 1).wait_recv()
                if not last or d == h:
                    ag_copy(d, h, s, last).start()
        for d in range(2):
            sib_copy(s, d).start()
        acc[...] += gather(s, 0, 0) + gather(s, 1, 0)
        for d in range(2):
            sib_copy(s, d).wait_recv()
        acc[...] += gather(s, 0, 1) + gather(s, 1, 1)

    def gather_loop(s, c):
        gather_step(s, False)
        return c

    lax.fori_loop(1, far - 1, gather_loop, 0)
    gather_step(far - 1, True)
    for d in range(2):
        ag_copy(d, d, far - 1, True).wait_recv()
    sib_copy(far, 0).start()
    acc[...] += gather(far, 0, 0)
    sib_copy(far, 0).wait_recv()
    found = (acc[...] + gather(far, 0, 1)).astype(BF)
    fine_ref[...] = (hid[...].astype(F32) + dot(found, w_down[...])).astype(BF)

    for l in range(ROUNDS):
        for c in halo(l):
            c.wait_send()
    row_copy.wait_send()
    for i in range(4):
        msg_copy(i).wait_send()

    def drain_counts(j, c):
        count_copy((me + j) % n, me).wait_send()
        return c

    lax.fori_loop(1, n, drain_counts, 0)

    for d in range(2):
        red_copy(d, d, 0).wait_send()
        ag_copy(d, d, far - 1, True).wait_send()
    sib_copy(0, 0).wait_send()
    sib_copy(far, 0).wait_send()

    def drain_ring(s, c):
        for d in range(2):
            for h in range(2):
                red_copy(d, h, s).wait_send()
                ag_copy(d, h, s - 1).wait_send()
            sib_copy(s, d).wait_send()
        return c

    lax.fori_loop(1, far, drain_ring, 0)


def shards(n, node_feat, coarse_feat, neighbors, up_owner, up_local, *weights):
    rows, width = node_feat.shape
    cells = coarse_feat.shape[0]
    edges = neighbors.shape[1]
    blocks = rows // BLOCK
    window = BLOCK + 2 * R
    far = n // 4
    half = cells // 2
    operands = (node_feat, coarse_feat, neighbors) + weights
    parent = up_owner[:, 0] * cells + up_local
    dma = pltpu.SemaphoreType.DMA
    vmem = pl.BlockSpec(memory_space=pltpu.VMEM)
    return pl.pallas_call(
        functools.partial(kernel, n),
        out_shape=(
            jax.ShapeDtypeStruct((rows, width), BF),
            jax.ShapeDtypeStruct((cells, width), BF),
        ),
        in_specs=[vmem] * 2 + [pl.BlockSpec(memory_space=pl.ANY)] * 12,
        out_specs=(vmem, vmem),
        scratch_shapes=[pltpu.VMEM(a.shape, a.dtype) for a in operands]
        + [
            dma((len(operands),)),
            pltpu.VMEM((blocks, edges * BLOCK, window), BF),
            pltpu.VMEM((ROUNDS, rows + 2 * R, width), BF),
            pltpu.VMEM((rows, width), F32),
            pltpu.VMEM((rows, width), BF),
            pltpu.VMEM((rows, width), BF),
            pltpu.VMEM((2, rows, width), BF),
            pltpu.VMEM((1, rows), jnp.int32),
            pltpu.VMEM((8 * n, cells), F32),
            pltpu.VMEM((8 * n, cells), F32),
            pltpu.VMEM((far, 2, 2, half, width), BF),
            pltpu.VMEM((far, 2, 2, half, width), BF),
            pltpu.VMEM((2, far + 1, 2, 2, half, width), BF),
            pltpu.VMEM((rows, width), F32),
            dma((ROUNDS, 2)),
            dma((ROUNDS, 2)),
            dma((n,)),
            dma((n,)),
            dma,
            dma,
            dma((4,)),
            dma((4,)),
            dma((far, 2, 2)),
            dma((far, 2, 2)),
            dma((far, 2, 2)),
            dma((far, 2, 2)),
            dma((far + 1, 2)),
            dma((far + 1, 2)),
        ],
        compiler_params=pltpu.CompilerParams(
            collective_id=0, has_side_effects=True, vmem_limit_bytes=60 * 1024 * 1024
        ),
    )(
        parent[:, None],
        parent[None, :],
        *operands,
    )


def solution(mesh):
    both = P(("groups", "mesh"), None)
    in_specs = (both, both, P("mesh", None), P("mesh", None), P("mesh")) + (P(),) * 9
    return jax.shard_map(
        functools.partial(shards, mesh.shape["mesh"]),
        mesh=mesh,
        in_specs=in_specs,
        out_specs=(both, both),
        check_vma=False,
    )
```

```python
import functools

import jax
import jax.numpy as jnp
from jax import lax
from jax.experimental import pallas as pl
from jax.experimental.pallas import tpu as pltpu
from jax.sharding import PartitionSpec as P

R = 128
ROUNDS = 2
BLOCK = 128
LOAD_ORDER = (0, 4, 3, 2, 8, 5, 6, 7, 9, 1, 10, 11)
BF = jnp.bfloat16
F32 = jnp.float32


def dot(a, b):
    return jnp.dot(a, b, preferred_element_type=F32)


def silu(x):
    h = 0.5 * x
    return h + h * jnp.tanh(h)


def kernel(
    n,
    own_ref,
    loc_ref,
    *refs,
):
    given, (fine_ref, coarse_ref), held = refs[:12], refs[12:14], refs[14:26]
    sweep(n, own_ref, loc_ref, given, held, *held, fine_ref, coarse_ref, *refs[26:])


def sweep(
    n,
    own_ref,
    loc_ref,
    given,
    held,
    x_ref,
    cf_ref,
    nb_ref,
    w_src,
    w_dst,
    w_node,
    w_edge,
    w_mix,
    bias_ref,
    w_up,
    w_coarse,
    w_down,
    fine_ref,
    coarse_ref,
    load_s,
    pr_ref,
    pc_ref,
    pick,
    ext,
    srch,
    esum,
    hid,
    msg,
    sib_row,
    hist,
    counts,
    sbuf,
    rbuf,
    gath,
    acc,
    halo_s,
    halo_r,
    cnt_s,
    cnt_r,
    row_s,
    row_r,
    msg_s,
    msg_r,
    red_s,
    red_r,
    ag_s,
    ag_r,
    sib_s,
    sib_r,
):
    rows, width = x_ref.shape
    edges = nb_ref.shape[0]
    cells = cf_ref.shape[0]
    half = cells // 2
    blocks = rows // BLOCK
    window = BLOCK + 2 * R
    ring = n // 2
    total = rows * n
    me = lax.axis_index("mesh")
    core = me % 2
    sibling = me + 1 - 2 * core
    chip = me // 2
    span = ring // 2
    pos = jnp.where(chip % 2 == 0, chip // 2, ring - 1 - chip // 2)

    def owner_at(place):
        place = (place + 2 * ring) % ring
        return jnp.where(place < span, 2 * place, 2 * (ring - 1 - place) + 1) * 2

    right = owner_at(pos + 1) + core
    left = owner_at(pos - 1) + core
    after = (me + 1) % n
    before = (me + n - 1) % n

    def remote(src, dst, ssem, rsem, dev):
        return pltpu.make_async_remote_copy(
            src_ref=src,
            dst_ref=dst,
            send_sem=ssem,
            recv_sem=rsem,
            device_id={"mesh": dev},
            device_id_type=pl.DeviceIdType.MESH,
        )

    barrier = pltpu.get_barrier_semaphore()

    def greet(j, c):
        pl.semaphore_signal(
            barrier,
            inc=1,
            device_id={"mesh": (me + j) % n},
            device_id_type=pl.DeviceIdType.MESH,
        )
        return c

    loads = [pltpu.make_async_copy(a, b, load_s.at[i]) for i, (a, b) in enumerate(zip(given, held))]
    for i in LOAD_ORDER:
        loads[i].start()
    lax.fori_loop(1, n, greet, 0)
    for i in LOAD_ORDER:
        loads[i].wait()

    ext[0, pl.ds(R, rows), :] = dot(x_ref[...], w_dst[0]).astype(BF)
    square = lax.broadcasted_iota(jnp.int32, (BLOCK, BLOCK), 0) == lax.broadcasted_iota(
        jnp.int32, (BLOCK, BLOCK), 1
    )

    def upright(row):
        return jnp.sum(jnp.where(square, row.astype(F32), 0.0), axis=1, keepdims=True).astype(
            jnp.int32
        )

    pr_ref[...] = own_ref[...] * cells + loc_ref[...]
    for b in range(blocks):
        part = slice(b * BLOCK, (b + 1) * BLOCK)
        pc_ref[part, :] = upright(pr_ref[:, part])
    lows = (lax.broadcasted_iota(jnp.int32, (8 * n, 1), 0) // 8) * cells
    parents = pr_ref[...]
    owner_hot = jnp.where((parents >= lows) & (parents < lows + cells), 1.0, 0.0).astype(BF)
    local = jnp.bitwise_and(pc_ref[...], cells - 1)
    local_hot = jnp.where(
        local == lax.broadcasted_iota(jnp.int32, (rows, cells), 1), 1.0, 0.0
    ).astype(BF)
    hist[...] = dot(owner_hot, local_hot)

    def build(b, c):
        r0 = b * BLOCK
        rel = nb_ref[:, pl.ds(pl.multiple_of(r0, BLOCK), BLOCK)] - (me * rows - R)
        rel = jnp.where(rel < 0, rel + total, rel)
        rel = jnp.where(rel >= total, rel - total, rel) - r0
        lanes = lax.broadcasted_iota(jnp.int32, (BLOCK, window), 1)
        for k in range(edges):
            pick[b, pl.ds(k * BLOCK, BLOCK), :] = jnp.where(
                upright(rel[k : k + 1, :]) == lanes, 0.5, 0.0
            ).astype(BF)
        return c

    def edge_block(l, b):
        r0 = b * BLOCK
        if l == 0:
            build(b, 0)
        sel = dot(pick[b], ext[l, pl.ds(r0, window), :])
        base = srch[pl.ds(r0, BLOCK), :]
        out = jnp.zeros((BLOCK, width), F32)
        for k in range(edges):
            h = base + sel[k * BLOCK : (k + 1) * BLOCK]
            out = out + (h + h * jnp.tanh(h))
        esum[pl.ds(r0, BLOCK), :] = out.astype(BF)

    def inner(l, low, high):
        def step(b, c):
            edge_block(l, b)
            return c

        lax.fori_loop(low, high, step, 0)

    def src_terms(l):
        here = x_ref if l == 0 else hid
        srch[...] = 0.5 * (dot(here[...], w_src[l]) + bias_ref[l : l + 1, :])

    early = blocks - 1 - (blocks - 2) // 6
    src_terms(0)
    inner(0, 1, early)

    pl.semaphore_wait(barrier, n - 1)

    def halo(l):
        return (
            remote(
                ext.at[l, pl.ds(R, R)],
                ext.at[l, pl.ds(R + rows, R)],
                halo_s.at[l, 0],
                halo_r.at[l, 0],
                before,
            ),
            remote(
                ext.at[l, pl.ds(rows, R)],
                ext.at[l, pl.ds(0, R)],
                halo_s.at[l, 1],
                halo_r.at[l, 1],
                after,
            ),
        )

    for c in halo(0):
        c.start()
    row_copy = remote(pr_ref, sib_row, row_s, row_r, sibling)
    row_copy.start()

    def count_copy(peer, slot):
        return remote(
            hist.at[pl.ds(peer * 8, 8)],
            counts.at[pl.ds(slot * 8, 8)],
            cnt_s.at[peer],
            cnt_r.at[slot],
            peer,
        )

    def send_counts(j, c):
        count_copy((me + j) % n, me).start()
        return c

    lax.fori_loop(1, n, send_counts, 0)

    chunk = rows // 4

    def msg_copy(i):
        part = pl.ds(i * chunk, chunk)
        return remote(msg.at[0, part], msg.at[1, part], msg_s.at[i], msg_r.at[i], sibling)

    for l in range(ROUNDS):
        here = x_ref if l == 0 else hid
        if l == 0:
            inner(0, early, blocks - 1)
        else:
            src_terms(l)
            inner(l, 1, blocks - 1)
        for c in halo(l):
            c.wait_recv()

        def outer(j, c, l=l):
            edge_block(l, j * (blocks - 1))
            return c

        lax.fori_loop(0, 2, outer, 0)
        for i in range(4):
            part = pl.ds(i * chunk, chunk)
            old = here[part, :]
            upd = silu(dot(old, w_node[l]) + dot(esum[part, :], w_edge[l])).astype(BF)
            new = (old.astype(F32) + dot(upd, w_mix[l])).astype(BF)
            hid[part, :] = new
            if l + 1 < ROUNDS:
                ext[l + 1, pl.ds(R + i * chunk, chunk), :] = dot(new, w_dst[l + 1]).astype(BF)
            else:
                msg[0, part, :] = silu(dot(new, w_up[...])).astype(BF)
                msg_copy(i).start()
        if l + 1 < ROUNDS:
            for c in halo(l + 1):
                c.start()

    counts[pl.ds(pl.multiple_of(me * 8, 8), 8), :] = hist[pl.ds(pl.multiple_of(me * 8, 8), 8), :]

    def take_counts(j, c):
        count_copy(me, (me + j) % n).wait_recv()
        return c

    lax.fori_loop(1, n, take_counts, 0)
    number = jnp.zeros((8, cells), F32)
    for j in range(n):
        number = number + counts[j * 8 : (j + 1) * 8, :]
    diag = lax.broadcasted_iota(jnp.int32, (cells, cells), 0) == lax.broadcasted_iota(
        jnp.int32, (cells, cells), 1
    )
    number = jnp.sum(jnp.where(diag, number[0:1, :], 0.0), axis=1, keepdims=True)
    scale = 1.0 / jnp.maximum(number, 1.0)

    row_copy.wait_recv()
    for i in range(4):
        msg_copy(i).wait_recv()

    far = ring // 2
    cell_iota = lax.broadcasted_iota(jnp.int32, (cells, 1), 0)
    parts = (slice(0, half), slice(half, cells))

    def partial_sums(place):
        ids = cell_iota + (owner_at(place) + core) * cells
        mine = jnp.where(pr_ref[...] == ids, 1.0, 0.0).astype(BF)
        theirs = jnp.where(sib_row[...] == ids, 1.0, 0.0).astype(BF)
        return dot(mine, msg[0]) + dot(theirs, msg[1])

    def red_copy(d, h, s):
        return remote(
            sbuf.at[s, d, h],
            rbuf.at[s, d, h],
            red_s.at[s, d, h],
            red_r.at[s, d, h],
            right if d == 0 else left,
        )

    def reduce_step(s, first):
        own = (partial_sums(pos + (far - s)), partial_sums(pos - (far - s)))
        pieces = ((0, 1), (1, 0), (0, 0), (1, 1))
        for d, h in pieces:
            part = own[d][parts[h]]
            if not (first and d != h):
                red_copy(d, h, s - 1).wait_recv()
                part = part + rbuf[s - 1, d, h].astype(F32)
            sbuf[s, d, h] = part.astype(BF)
            red_copy(d, h, s).start()

    part = partial_sums(pos + far)
    for d in range(2):
        sbuf[0, d, d] = part[parts[d]].astype(BF)
        red_copy(d, d, 0).start()
    reduce_step(1, True)

    def reduce_loop(s, c):
        reduce_step(s, False)
        return c

    lax.fori_loop(2, far, reduce_loop, 0)
    part = partial_sums(pos)

    def ag_copy(d, h, s, last=False):
        return remote(
            gath.at[0, s, d, h],
            gath.at[0, s + 1, 0 if last else d, h],
            ag_s.at[s, d, h],
            ag_r.at[s, d, h],
            right if d == 0 else left,
        )

    def sib_copy(s, d):
        return remote(gath.at[0, s, d], gath.at[1, s, d], sib_s.at[s, d], sib_r.at[s, d], sibling)

    for h in (1, 0):
        summed = part[parts[h]]
        for d in range(2):
            red_copy(d, h, far - 1).wait_recv()
            summed = summed + rbuf[far - 1, d, h].astype(F32)
        mean = (summed * scale[parts[h]]).astype(BF)
        out = (cf_ref[parts[h], :].astype(F32) + dot(mean, w_coarse[...])).astype(BF)
        gath[0, 0, 0, h] = out
        gath[0, 0, 1, h] = out
        ag_copy(0, h, 0).start()
        ag_copy(1, h, 0).start()
        coarse_ref[parts[h], :] = out
    sib_copy(0, 0).start()

    lane_iota = lax.broadcasted_iota(jnp.int32, (1, cells), 1)

    def gather(s, d, slot):
        owner = owner_at(pos - s if d == 0 else pos + s) + (core if slot == 0 else 1 - core)
        hot = jnp.where(pc_ref[...] == lane_iota + owner * cells, 1.0, 0.0).astype(BF)
        return dot(hot, gath[slot, s, d].reshape(cells, width))

    acc[...] = gather(0, 0, 0)
    sib_copy(0, 0).wait_recv()
    acc[...] += gather(0, 0, 1)

    def gather_step(s, last):
        for h in (1, 0):
            for d in range(2):
                ag_copy(d, h, s - 1).wait_recv()
                if not last or d == h:
                    ag_copy(d, h, s, last).start()
        for d in range(2):
            sib_copy(s, d).start()
        acc[...] += gather(s, 0, 0) + gather(s, 1, 0)
        for d in range(2):
            sib_copy(s, d).wait_recv()
        acc[...] += gather(s, 0, 1) + gather(s, 1, 1)

    def gather_loop(s, c):
        gather_step(s, False)
        return c

    lax.fori_loop(1, far - 1, gather_loop, 0)
    gather_step(far - 1, True)
    for d in range(2):
        ag_copy(d, d, far - 1, True).wait_recv()
    sib_copy(far, 0).start()
    acc[...] += gather(far, 0, 0)
    sib_copy(far, 0).wait_recv()
    found = (acc[...] + gather(far, 0, 1)).astype(BF)
    fine_ref[...] = (hid[...].astype(F32) + dot(found, w_down[...])).astype(BF)

    for l in range(ROUNDS):
        for c in halo(l):
            c.wait_send()
    row_copy.wait_send()
    for i in range(4):
        msg_copy(i).wait_send()

    def drain_counts(j, c):
        count_copy((me + j) % n, me).wait_send()
        return c

    lax.fori_loop(1, n, drain_counts, 0)

    for d in range(2):
        red_copy(d, d, 0).wait_send()
        ag_copy(d, d, far - 1, True).wait_send()
    sib_copy(0, 0).wait_send()
    sib_copy(far, 0).wait_send()

    def drain_ring(s, c):
        for d in range(2):
            for h in range(2):
                red_copy(d, h, s).wait_send()
                ag_copy(d, h, s - 1).wait_send()
            sib_copy(s, d).wait_send()
        return c

    lax.fori_loop(1, far, drain_ring, 0)


def shards(n, node_feat, coarse_feat, neighbors, up_owner, up_local, *weights):
    rows, width = node_feat.shape
    cells = coarse_feat.shape[0]
    edges = neighbors.shape[1]
    blocks = rows // BLOCK
    window = BLOCK + 2 * R
    far = n // 4
    half = cells // 2
    operands = (node_feat, coarse_feat, neighbors.T) + weights
    dma = pltpu.SemaphoreType.DMA
    vmem = pl.BlockSpec(memory_space=pltpu.VMEM)
    return pl.pallas_call(
        functools.partial(kernel, n),
        out_shape=(
            jax.ShapeDtypeStruct((rows, width), BF),
            jax.ShapeDtypeStruct((cells, width), BF),
        ),
        in_specs=[vmem] * 2 + [pl.BlockSpec(memory_space=pl.ANY)] * 12,
        out_specs=(vmem, vmem),
        scratch_shapes=[pltpu.VMEM(a.shape, a.dtype) for a in operands]
        + [
            dma((len(operands),)),
            pltpu.VMEM((1, rows), jnp.int32),
            pltpu.VMEM((rows, 1), jnp.int32),
            pltpu.VMEM((blocks, edges * BLOCK, window), BF),
            pltpu.VMEM((ROUNDS, rows + 2 * R, width), BF),
            pltpu.VMEM((rows, width), F32),
            pltpu.VMEM((rows, width), BF),
            pltpu.VMEM((rows, width), BF),
            pltpu.VMEM((2, rows, width), BF),
            pltpu.VMEM((1, rows), jnp.int32),
            pltpu.VMEM((8 * n, cells), F32),
            pltpu.VMEM((8 * n, cells), F32),
            pltpu.VMEM((far, 2, 2, half, width), BF),
            pltpu.VMEM((far, 2, 2, half, width), BF),
            pltpu.VMEM((2, far + 1, 2, 2, half, width), BF),
            pltpu.VMEM((rows, width), F32),
            dma((ROUNDS, 2)),
            dma((ROUNDS, 2)),
            dma((n,)),
            dma((n,)),
            dma,
            dma,
            dma((4,)),
            dma((4,)),
            dma((far, 2, 2)),
            dma((far, 2, 2)),
            dma((far, 2, 2)),
            dma((far, 2, 2)),
            dma((far + 1, 2)),
            dma((far + 1, 2)),
        ],
        compiler_params=pltpu.CompilerParams(
            collective_id=0, has_side_effects=True, vmem_limit_bytes=60 * 1024 * 1024
        ),
    )(
        up_owner.reshape(1, rows),
        up_local.reshape(1, rows),
        *operands,
    )


def solution(mesh):
    both = P(("groups", "mesh"), None)
    in_specs = (both, both, P("mesh", None), P("mesh", None), P("mesh")) + (P(),) * 9
    return jax.shard_map(
        functools.partial(shards, mesh.shape["mesh"]),
        mesh=mesh,
        in_specs=in_specs,
        out_specs=(both, both),
        check_vma=False,
    )
```
